512 devices in a mesh: cfg: 2 (over z_hi), batch: 32 (over z_lo, x, core), seq: 8 (over y).
Axes of the slice: x: 4, y: 8, z: 8 (z_hi: 2, z_lo: 4; z = z_hi * 4 + z_lo), core: 2. Of those that a mesh axis runs over, the one named last changes fastest.
Arguments:
- query_rows: bfloat16 [2, 40960, 4096], P('cfg', ('batch', 'seq')), parts along dimension 1, may hold values from -32 to 32
- key_rows: bfloat16 [2, 40960, 4096], P('cfg', ('batch', 'seq')), parts along dimension 1, may hold values from -32 to 32
- value_rows: bfloat16 [2, 40960, 4096], P('cfg', ('batch', 'seq')), parts along dimension 1, may hold values from -6 to 6
- query_gain: float32 [4096], replicated, may hold values from 0.25 to 1.75
- key_gain: float32 [4096], replicated, may hold values from 0.25 to 1.75
- out_map: bfloat16 [4096, 64], replicated, may hold values from -0.09375 to 0.09375
- latents: float32 [40960, 64], P(('batch', 'seq')), parts along dimension 0, may hold values from -6 to 6
- step_index: int32 [1], replicated, may hold values from 0 to 49
Outputs:
- next_latents: float32 [40960, 64], P(('batch', 'seq')), parts along dimension 0
- denoised: float32 [40960, 64], P(('batch', 'seq')), parts along dimension 0
The draws below stay inside these ranges and needn't reach their ends.
There are 32 independent parts, one for each index of `batch`. The reference program is written for one: setup_inputs(seed, part) draws one part's arguments, and reference() takes and returns one part's arrays. A program takes and returns all parts, laid end to end along the dimension named above; an argument that names none is the same for every part. Nothing has to cross between parts.
All inputs are finite; a program needn't handle non-finite values.
Results may differ from the reference program's by a relative error of at most 0.0025.
The reference program's roundings to bfloat16 on the way count: a program that leaves them out, or rounds other values in their place, can miss the bound.
Values may be sent and summed in bfloat16 or wider, within the bound.
No kernel may reach another device: no remote copies, remote signals or barrier semaphores. Data moves between devices by JAX's collectives and lax.ppermute only.
A program may use at most 64 MiB of HBM per device.

```python
import math
import jax
import jax.numpy as jnp
from jax import lax

HEADS = 32
HEAD_DIM = 128
CHANNELS = 64
STEPS = 50
SEQ_LEN = 1280
FEATURES = 4096


def field_scales(key, column_top):
    key_one, key_two = jax.random.split(key)
    column = jnp.exp(jax.random.uniform(key_one, (1, 1, FEATURES)) * math.log(column_top))
    row_scale = jnp.exp(jax.random.uniform(key_two, (2, SEQ_LEN, 1)) * math.log(10.0))
    return column * row_scale


def draw_query_rows(key, part):
    key = jax.random.fold_in(key, 11)
    key_one, key_two = jax.random.split(key, 2)
    raw_field = jax.random.normal(key_one, (2, SEQ_LEN, FEATURES), jnp.float32)
    drawn = raw_field * field_scales(key_two, 10.0)
    return jnp.clip(drawn, -32.0, 32.0).astype(jnp.bfloat16)


def draw_key_rows(key, part):
    key = jax.random.fold_in(key, 12)
    key_one, key_two = jax.random.split(key, 2)
    raw_field = jax.random.normal(key_one, (2, SEQ_LEN, FEATURES), jnp.float32)
    drawn = raw_field * field_scales(key_two, 10.0)
    return jnp.clip(drawn, -32.0, 32.0).astype(jnp.bfloat16)


def block_levels(own_key, dims, cuts, low, top_value):
    def one(dim, parts):
        steps = jax.random.uniform(jax.random.fold_in(jax.random.fold_in(own_key, 6), dim), (parts,), jnp.float32, low / len(cuts), top_value / len(cuts))
        return jnp.repeat(jnp.exp(steps), dims[dim] // parts).reshape((-1,) + (1,) * (len(dims) - dim - 1))

    loudness = one(*cuts[0])
    for cut in cuts[1:]:
        loudness = loudness * one(*cut)
    return loudness


def scatter_about(stream_key, shape, width, reach, cuts=(), dtype=jnp.bfloat16):
    array = width * jax.random.normal(stream_key, shape, jnp.float32)
    if cuts:
        array = array * block_levels(stream_key, shape, cuts, -0.22, 0.18)
    return jnp.clip(array, -reach, reach).astype(dtype)


def setup_inputs(seed: int = 0, part: int = 0) -> dict:
    splits = jax.random.split(jax.random.key(seed), 9)
    own_keys = jax.random.split(jax.random.fold_in(splits[8], part), 9)
    query_rows = draw_query_rows(jax.random.fold_in(jax.random.fold_in(splits[8], part), 71), part)
    key_rows = draw_key_rows(jax.random.fold_in(jax.random.fold_in(splits[8], part), 71), part)
    value_rows = scatter_about(own_keys[2], (2, SEQ_LEN, FEATURES), 1.0, 6.0, ((0, 2), (1, 8)))
    query_gain = jnp.clip(1.0 + 0.15 * jax.random.normal(splits[3], (FEATURES,), jnp.float32), 0.25, 1.75)
    key_gain = jnp.clip(1.0 + 0.15 * jax.random.normal(splits[4], (FEATURES,), jnp.float32), 0.25, 1.75)
    out_map = scatter_about(splits[5], (FEATURES, CHANNELS), FEATURES ** -0.5, 0.09375)
    latents = scatter_about(own_keys[6], (SEQ_LEN, CHANNELS), 1.0, 6.0, ((0, 8),), jnp.float32)
    step_index = jax.random.randint(splits[7], (1,), 0, STEPS).astype(jnp.int32)
    return {"query_rows": query_rows, "key_rows": key_rows, "value_rows": value_rows, "query_gain": query_gain, "key_gain": key_gain, "out_map": out_map, "latents": latents, "step_index": step_index}


GUIDANCE = 5.0
FLOW_SHIFT = 5.0
EPSILON = 1e-06

def normalize(rows_in, gain_row):
    values = rows_in.astype(jnp.float32)
    mean_square = lax.optimization_barrier(jnp.mean(values * values, axis=-1, keepdims=True))
    return (values * lax.rsqrt(mean_square + EPSILON) * gain_row).astype(jnp.bfloat16)

def sigma_at(progress):
    remain = 1.0 - progress / STEPS
    return FLOW_SHIFT * remain / (1.0 + (FLOW_SHIFT - 1.0) * remain)

def head_attention(head_parts):
    query_head, key_head, value_head = head_parts
    scores = jnp.dot(query_head, key_head.T, preferred_element_type=jnp.float32) * (1.0 / math.sqrt(HEAD_DIM))
    row_top = lax.optimization_barrier(jnp.max(scores, axis=-1, keepdims=True))
    weights = jnp.exp(scores - row_top)
    weights_bf = (weights / lax.optimization_barrier(jnp.sum(weights, axis=-1, keepdims=True))).astype(jnp.bfloat16)
    return jnp.dot(weights_bf, value_head, preferred_element_type=jnp.float32).astype(jnp.bfloat16)

def heads_first(rows_in):
    return rows_in.reshape(SEQ_LEN, HEADS, HEAD_DIM).transpose(1, 0, 2)

def branch_attention(query_branch, key_branch, value_branch):
    attended = lax.map(head_attention, (heads_first(query_branch), heads_first(key_branch), heads_first(value_branch)))
    return attended.transpose(1, 0, 2).reshape(SEQ_LEN, FEATURES)

def reference(query_rows, key_rows, value_rows, query_gain, key_gain, out_map, latents, step_index):
    query_normed = normalize(query_rows, query_gain)
    key_normed = normalize(key_rows, key_gain)
    velocities = []
    for branch in range(2):
        attended = branch_attention(query_normed[branch], key_normed[branch], value_rows[branch])
        velocities.append(jnp.dot(attended, out_map, preferred_element_type=jnp.float32))
    guided = velocities[1] + GUIDANCE * (velocities[0] - velocities[1])
    progress = step_index[0].astype(jnp.float32)
    sigma_now = sigma_at(progress)
    sigma_next = sigma_at(progress + 1.0)
    return (latents + (sigma_next - sigma_now) * guided, latents - sigma_now * guided)
```

```python
import functools
import math

import jax
import jax.numpy as jnp
from jax import lax
from jax.experimental import pallas as pl
from jax.experimental.pallas import tpu as pltpu
from jax.sharding import PartitionSpec as P

HEADS = 32
HEAD_DIM = 128
CHANNELS = 64
STEPS = 50
GUIDANCE = 5.0
FLOW_SHIFT = 5.0
EPSILON = 1e-06
VMEM_LIMIT = 48 * 1024 * 1024


def sigma_at(progress):
    remain = 1.0 - progress / STEPS
    return FLOW_SHIFT * remain / (1.0 + (FLOW_SHIFT - 1.0) * remain)


def params():
    return pltpu.CompilerParams(vmem_limit_bytes=VMEM_LIMIT)


def normed(rows_ref, gain_ref):
    values = rows_ref[...].astype(jnp.float32)
    mean_square = jnp.mean(values * values, axis=-1, keepdims=True)
    return (values * lax.rsqrt(mean_square + EPSILON) * gain_ref[...]).astype(jnp.bfloat16)


def pack_kv_kernel(groups, key_ref, value_ref, gain_ref, map_ref, out_ref):
    width = key_ref.shape[1] // groups
    key_normed = normed(key_ref, gain_ref)
    pair = 2 * HEAD_DIM
    row = lax.broadcasted_iota(jnp.int32, (pair, 2 * CHANNELS), 0)
    lane = lax.broadcasted_iota(jnp.int32, (pair, 2 * CHANNELS), 1)
    same_head = (row < HEAD_DIM) == (lane < CHANNELS)
    for group in range(groups):
        out_ref[group, :, :width] = key_normed[:, group * width : (group + 1) * width]
        for step in range(width // pair):
            first = group * width + step * pair
            columns = map_ref[first : first + pair, :]
            both = jnp.concatenate([columns, columns], axis=1)
            both = jnp.where(same_head, both, jnp.zeros_like(both))
            mapped = jnp.dot(
                value_ref[:, first : first + pair], both, preferred_element_type=jnp.float32
            )
            left = width + step * 2 * CHANNELS
            out_ref[group, :, left : left + 2 * CHANNELS] = mapped.astype(jnp.bfloat16)


def pack_kv(key_rows, value_rows, gain, out_map, groups, blocks=2):
    rows, features = key_rows.shape
    width = features // groups
    packed = width + width // HEAD_DIM * CHANNELS
    step = rows // blocks
    return pl.pallas_call(
        functools.partial(pack_kv_kernel, groups),
        out_shape=jax.ShapeDtypeStruct((groups, rows, packed), jnp.bfloat16),
        grid=(blocks,),
        in_specs=[
            pl.BlockSpec((step, features), lambda i: (i, 0)),
            pl.BlockSpec((step, features), lambda i: (i, 0)),
            pl.BlockSpec((1, features), lambda i: (0, 0)),
            pl.BlockSpec((features, CHANNELS), lambda i: (0, 0)),
        ],
        out_specs=pl.BlockSpec((groups, step, packed), lambda i: (0, i, 0)),
        compiler_params=params(),
        cost_estimate=pl.CostEstimate(flops=2**28, bytes_accessed=5 * 2**20, transcendentals=0),
        name="pack_kv",
    )(key_rows, value_rows, gain, out_map)


def pack_q_kernel(groups, place_ref, query_ref, gain_ref, *refs):
    out_refs, scratch = refs[:groups], refs[groups]
    width = query_ref.shape[1] // groups
    scratch[...] = normed(query_ref, gain_ref)
    place = place_ref[0]
    for e in range(groups):
        first = pl.multiple_of(jnp.bitwise_xor(place, e) * width, width)
        out_refs[e][...] = scratch[:, pl.ds(first, width)]


def pack_q(place, query_rows, gain, groups, blocks=2):
    rows, features = query_rows.shape
    width = features // groups
    step = rows // blocks
    return pl.pallas_call(
        functools.partial(pack_q_kernel, groups),
        out_shape=[jax.ShapeDtypeStruct((rows, width), jnp.bfloat16)] * groups,
        grid=(blocks,),
        in_specs=[
            pl.BlockSpec(memory_space=pltpu.SMEM),
            pl.BlockSpec((step, features), lambda i: (i, 0)),
            pl.BlockSpec((1, features), lambda i: (0, 0)),
        ],
        out_specs=[pl.BlockSpec((step, width), lambda i: (i, 0))] * groups,
        scratch_shapes=[pltpu.VMEM((step, features), jnp.bfloat16)],
        compiler_params=params(),
        cost_estimate=pl.CostEstimate(flops=2**24, bytes_accessed=5 * 2**19, transcendentals=0),
        name="pack_q",
    )(place, query_rows, gain)


def attend_kernel(count, *refs):
    query_refs, kv_ref, out_ref = refs[:count], refs[count], refs[count + 1]
    width = query_refs[0].shape[1]
    rows = query_refs[0].shape[0]
    factor = math.log2(math.e) / math.sqrt(HEAD_DIM)
    left_half = lax.broadcasted_iota(jnp.int32, (1, 2 * CHANNELS), 1) < CHANNELS
    for block in range(count):
        total = None
        for pair in range(width // (2 * HEAD_DIM)):
            terms = []
            for head in (2 * pair, 2 * pair + 1):
                lanes = slice(head * HEAD_DIM, (head + 1) * HEAD_DIM)
                scores = lax.dot_general(
                    query_refs[block][:, lanes],
                    kv_ref[:, lanes],
                    (((1,), (1,)), ((), ())),
                    preferred_element_type=jnp.float32,
                )
                top = jnp.max(scores, axis=-1, keepdims=True)
                weights = jnp.exp2((scores - top) * factor)
                inverse = 1.0 / jnp.sum(weights, axis=-1, keepdims=True)
                left = width + pair * 2 * CHANNELS
                terms.append(
                    jnp.dot(
                        (weights * inverse).astype(jnp.bfloat16),
                        kv_ref[:, left : left + 2 * CHANNELS],
                        preferred_element_type=jnp.float32,
                    )
                )
            term = jnp.where(left_half, terms[0], terms[1])
            total = term if total is None else total + term
        total = total + pltpu.roll(total, CHANNELS, 1)
        half = rows // 2
        out_ref[block] = jnp.where(left_half, total[:half], total[half:])


def attend(queries, kv):
    count = len(queries)
    rows, width = queries[0].shape
    keys = kv.shape[0]
    work = count * rows * keys * (width // HEAD_DIM)
    return pl.pallas_call(
        functools.partial(attend_kernel, count),
        out_shape=jax.ShapeDtypeStruct((count, rows // 2, 2 * CHANNELS), jnp.float32),
        in_specs=[pl.BlockSpec(memory_space=pltpu.VMEM)] * (count + 1),
        out_specs=pl.BlockSpec(memory_space=pltpu.VMEM),
        compiler_params=params(),
        cost_estimate=pl.CostEstimate(
            flops=work * 4 * HEAD_DIM, bytes_accessed=2 * kv.size, transcendentals=work
        ),
        name="attend",
    )(*queries, kv)


def local(query_rows, key_rows, value_rows, query_gain, key_gain, out_map, latents, step_index):
    groups = lax.axis_size("seq")
    place = lax.axis_index("seq").astype(jnp.int32).reshape(1)
    rows = query_rows.shape[1]

    def exchange(array, e):
        return lax.ppermute(array, "seq", [(i, i ^ e) for i in range(groups)])

    kv_mine = pack_kv(key_rows[0], value_rows[0], key_gain.reshape(1, -1), out_map, groups)
    kv = lax.all_to_all(kv_mine, "seq", split_axis=0, concat_axis=0, tiled=True)
    kv = kv.reshape(groups * rows, kv.shape[2])
    query_parts = pack_q(place, query_rows[0], query_gain.reshape(1, -1), groups)
    held = {0: query_parts[0]}
    for e in (4, 5, 6, 7, 3, 2, 1):
        held[e] = exchange(query_parts[e], e)

    own = attend([held[0]], kv)[0]
    far = [attend([held[e]], kv) for e in (4, 5, 6, 7)]
    from_far = exchange(jnp.concatenate(far, axis=0), 4)
    second = [attend([held[e]], kv)[0] for e in (2, 3)]
    from_second = exchange(
        jnp.stack([second[0] + from_far[2], second[1] + from_far[3]]), 2
    )
    last = attend([held[1]], kv)[0]
    from_last = exchange(last + from_far[1] + from_second[1], 1)
    total = own + from_far[0] + from_second[0] + from_last

    share = jnp.where(lax.axis_index("cfg") == 0, GUIDANCE, 1.0 - GUIDANCE)
    total = total * share
    total = total + lax.ppermute(total, "cfg", [(0, 1), (1, 0)])
    guided = jnp.concatenate([total[:, :CHANNELS], total[:, CHANNELS:]], axis=0)

    progress = step_index[0].astype(jnp.float32)
    sigma_now = sigma_at(progress)
    sigma_next = sigma_at(progress + 1.0)
    return (latents + (sigma_next - sigma_now) * guided, latents - sigma_now * guided)


def solution(mesh):
    placed = (
        P("cfg", ("batch", "seq"), None),
        P("cfg", ("batch", "seq"), None),
        P("cfg", ("batch", "seq"), None),
        P(),
        P(),
        P(),
        P(("batch", "seq"), None),
        P(),
    )
    return jax.shard_map(
        local,
        mesh=mesh,
        in_specs=placed,
        out_specs=(P(("batch", "seq"), None), P(("batch", "seq"), None)),
        check_vma=False,
    )
```

```python
import functools
import math

import jax
import jax.numpy as jnp
from jax import lax
from jax.experimental import pallas as pl
from jax.experimental.pallas import tpu as pltpu
from jax.sharding import PartitionSpec as P

HEADS = 32
HEAD_DIM = 128
CHANNELS = 64
STEPS = 50
GUIDANCE = 5.0
FLOW_SHIFT = 5.0
EPSILON = 1e-06
VMEM_LIMIT = 24 * 1024 * 1024
PACK_VMEM_LIMIT = 60 * 1024 * 1024


def sigma_at(progress):
    remain = 1.0 - progress / STEPS
    return FLOW_SHIFT * remain / (1.0 + (FLOW_SHIFT - 1.0) * remain)


def params(limit=VMEM_LIMIT):
    return pltpu.CompilerParams(vmem_limit_bytes=limit)


def normed(values, gain):
    values = values.astype(jnp.float32)
    mean_square = jnp.mean(values * values, axis=-1, keepdims=True)
    return (values * lax.rsqrt(mean_square + EPSILON) * gain).astype(jnp.bfloat16)


def mapped_pair(values, map_ref, first):
    columns = map_ref[:, first : first + 2 * HEAD_DIM]
    none = jnp.zeros((CHANNELS, HEAD_DIM), jnp.bfloat16)
    both = jnp.concatenate(
        [
            jnp.concatenate([columns[:, :HEAD_DIM], none], axis=1),
            jnp.concatenate([none, columns[:, HEAD_DIM:]], axis=1),
        ],
        axis=0,
    )
    return lax.dot_general(
        values, both, (((1,), (1,)), ((), ())), preferred_element_type=jnp.float32
    ).astype(jnp.bfloat16)


def pack_kernel(groups, late, pieces, place_ref, *refs):
    outs = 1 if not late else groups
    sources, gains, map_hbm = refs[:3], refs[3:5], refs[5]
    out_refs = refs[6 : 6 + outs]
    held, gain_refs, map_ref, stage, in_sems, small_sems, out_sems = refs[6 + outs :]
    rows, features = sources[0].shape
    width = features // groups
    head_part = width - HEAD_DIM
    step = rows // pieces
    small = [
        pltpu.make_async_copy(gains[0], gain_refs.at[0], small_sems.at[0]),
        pltpu.make_async_copy(gains[1], gain_refs.at[1], small_sems.at[1]),
        pltpu.make_async_copy(map_hbm, map_ref, small_sems.at[2]),
    ]
    loads = [
        [
            pltpu.make_async_copy(
                sources[which].at[pl.ds(piece * step, step)],
                held.at[which, pl.ds(piece * step, step)],
                in_sems.at[which, piece],
            )
            for which in range(3)
        ]
        for piece in range(pieces)
    ]
    for load in loads[0] + small:
        load.start()
    for piece in loads[1:]:
        for load in piece:
            load.start()
    for load in small:
        load.wait()
    place = place_ref[0]
    stores = []
    for piece in range(pieces):
        for load in loads[piece]:
            load.wait()
        at = slice(piece * step, (piece + 1) * step)
        query_normed = normed(held[0, at, :], gain_refs[0])
        key_normed = normed(held[1, at, :], gain_refs[1])
        for group in range(groups):
            start = group * width
            if late:
                first, last = start + head_part, start + width
                pair = start + 2 * HEAD_DIM
            else:
                first, last = start, start + head_part
                pair = start
            size = last - first
            stage[group, at, :size] = query_normed[:, first:last]
            stage[group, at, size : 2 * size] = key_normed[:, first:last]
            stage[group, at, 2 * size :] = mapped_pair(
                held[2, at, pair : pair + 2 * HEAD_DIM], map_ref, pair
            )
        there = pl.ds(piece * step, step)
        if late:
            for e in range(groups):
                store = pltpu.make_async_copy(
                    stage.at[jnp.bitwise_xor(place, e), there], out_refs[e].at[there], out_sems.at[piece, e]
                )
                store.start()
                stores.append(store)
        else:
            store = pltpu.make_async_copy(
                stage.at[:, there], out_refs[0].at[:, there], out_sems.at[piece, 0]
            )
            store.start()
            stores.append(store)
    for store in stores:
        store.wait()


def pack(place, query_rows, key_rows, value_rows, query_gain, key_gain, out_map, groups, late, pieces=2):
    rows, features = query_rows.shape
    heads = features // groups // HEAD_DIM
    packed = 2 * (1 if late else heads - 1) * HEAD_DIM + 2 * CHANNELS
    hbm = pl.BlockSpec(memory_space=pltpu.HBM)
    if late:
        out_shape = [pltpu.HBM((rows, packed), jnp.bfloat16)] * groups
    else:
        out_shape = [pltpu.HBM((groups, rows, packed), jnp.bfloat16)]
    return pl.pallas_call(
        functools.partial(pack_kernel, groups, late, pieces),
        out_shape=out_shape,
        in_specs=[pl.BlockSpec(memory_space=pltpu.SMEM)] + [hbm] * 6,
        out_specs=[hbm] * len(out_shape),
        scratch_shapes=[
            pltpu.VMEM((3, rows, features), jnp.bfloat16),
            pltpu.VMEM((2, 1, features), jnp.float32),
            pltpu.VMEM((CHANNELS, features), jnp.bfloat16),
            pltpu.VMEM((groups, rows, packed), jnp.bfloat16),
            pltpu.SemaphoreType.DMA((3, pieces)),
            pltpu.SemaphoreType.DMA((3,)),
            pltpu.SemaphoreType.DMA((pieces, groups)),
        ],
        compiler_params=params(PACK_VMEM_LIMIT),
        cost_estimate=pl.CostEstimate(flops=2**28, bytes_accessed=8 * 2**20, transcendentals=0),
        name="pack_late" if late else "pack_early",
    )(place, query_rows, key_rows, value_rows, query_gain, key_gain, out_map)


def scores_between(queries, keys):
    return lax.dot_general(
        queries, keys, (((1,), (1,)), ((), ())), preferred_element_type=jnp.float32
    )


def softmax_weights(scores):
    factor = math.log2(math.e) / math.sqrt(HEAD_DIM)
    top = jnp.max(scores, axis=-1, keepdims=True)
    weights = jnp.exp2((scores - top) * factor)
    return (weights * (1.0 / jnp.sum(weights, axis=-1, keepdims=True))).astype(jnp.bfloat16)


def left_half():
    return lax.broadcasted_iota(jnp.int32, (1, 2 * CHANNELS), 1) < CHANNELS


def early_kernel(chunk, data_ref, term_ref, weights_ref):
    heads = 3
    mapped = data_ref[:, 2 * heads * HEAD_DIM :]

    @pl.loop(0, data_ref.shape[0] // chunk)
    def _(index):
        rows = pl.ds(pl.multiple_of(index * chunk, chunk), chunk)
        terms = []
        for head in range(heads):
            lanes = slice(head * HEAD_DIM, (head + 1) * HEAD_DIM)
            keys = slice((heads + head) * HEAD_DIM, (heads + head + 1) * HEAD_DIM)
            weights = softmax_weights(scores_between(data_ref[rows, lanes], data_ref[:, keys]))
            if head < 2:
                terms.append(jnp.dot(weights, mapped, preferred_element_type=jnp.float32))
            else:
                weights_ref[rows, :] = weights
        term_ref[rows, :] = jnp.where(left_half(), terms[0], terms[1])


def late_kernel(chunk, groups, place_ref, term_ref, weights_ref, *refs):
    held_refs, out_ref, data_ref = refs[:groups], refs[groups], refs[groups + 1]
    part = held_refs[0].shape[0]
    place = place_ref[0]
    for e in range(groups):
        first = pl.multiple_of(jnp.bitwise_xor(place, e) * part, part)
        data_ref[pl.ds(first, part), :] = held_refs[e][...]
    half = part // 2
    mapped = data_ref[:, 2 * HEAD_DIM :]
    count = data_ref.shape[0] // chunk

    def scores_of(index):
        return scores_between(
            data_ref[index * chunk : (index + 1) * chunk, :HEAD_DIM], data_ref[:, HEAD_DIM : 2 * HEAD_DIM]
        )

    ahead = scores_of(0)
    for index in range(count):
        scores = ahead
        if index + 1 < count:
            ahead = scores_of(index + 1)
        rows = slice(index * chunk, (index + 1) * chunk)
        second = jnp.dot(weights_ref[rows, :], mapped, preferred_element_type=jnp.float32)
        third = jnp.dot(softmax_weights(scores), mapped, preferred_element_type=jnp.float32)
        total = term_ref[rows, :] + jnp.where(left_half(), second, third)
        total = total + pltpu.roll(total, CHANNELS, 1)
        for block in range(chunk // part):
            first = block * part
            out_ref[index * (chunk // part) + block] = jnp.where(
                left_half(), total[first : first + half], total[first + half : first + part]
            )


def attend_early(data, chunk=320):
    keys = data.shape[0]
    vmem = pl.BlockSpec(memory_space=pltpu.VMEM)
    return pl.pallas_call(
        functools.partial(early_kernel, chunk),
        out_shape=[
            jax.ShapeDtypeStruct((keys, 2 * CHANNELS), jnp.float32),
            jax.ShapeDtypeStruct((keys, keys), jnp.bfloat16),
        ],
        in_specs=[vmem],
        out_specs=[vmem, vmem],
        compiler_params=params(),
        cost_estimate=pl.CostEstimate(
            flops=8 * 10**9, bytes_accessed=2 * data.size, transcendentals=3 * keys * keys
        ),
        name="attend_early",
    )(data)


def attend_late(place, term, weights, held, chunk=320):
    groups = len(held)
    part, width = held[0].shape
    vmem = pl.BlockSpec(memory_space=pltpu.VMEM)
    return pl.pallas_call(
        functools.partial(late_kernel, chunk, groups),
        out_shape=jax.ShapeDtypeStruct((groups, part // 2, 2 * CHANNELS), jnp.float32),
        in_specs=[pl.BlockSpec(memory_space=pltpu.SMEM)] + [vmem] * (groups + 2),
        out_specs=vmem,
        scratch_shapes=[pltpu.VMEM((groups * part, width), jnp.bfloat16)],
        compiler_params=params(),
        cost_estimate=pl.CostEstimate(
            flops=3 * 10**9, bytes_accessed=2 * 10**6, transcendentals=(groups * part) ** 2
        ),
        name="attend_late",
    )(place, term, weights, *held)


def finish_kernel(index_ref, both_ref, latents_ref, next_ref, denoised_ref):
    progress = index_ref[0].astype(jnp.float32)
    sigma_now = sigma_at(progress)
    sigma_next = sigma_at(progress + 1.0)
    turned = (both_ref[0] + both_ref[1]).T
    guided = jnp.concatenate([turned[:CHANNELS], turned[CHANNELS:]], axis=1)
    latents = latents_ref[...]
    next_ref[...] = latents + (sigma_next - sigma_now) * guided
    denoised_ref[...] = latents - sigma_now * guided


def finish(step_index, both, latents):
    vmem = pl.BlockSpec(memory_space=pltpu.VMEM)
    return pl.pallas_call(
        finish_kernel,
        out_shape=[jax.ShapeDtypeStruct(latents.shape, latents.dtype)] * 2,
        in_specs=[pl.BlockSpec(memory_space=pltpu.SMEM), vmem, vmem],
        out_specs=[vmem, vmem],
        compiler_params=params(),
        cost_estimate=pl.CostEstimate(flops=2**16, bytes_accessed=2**17, transcendentals=0),
        name="finish",
    )(step_index, both, latents)


def local(query_rows, key_rows, value_rows, query_gain, key_gain, out_map, latents, step_index):
    groups = lax.axis_size("seq")
    place = lax.axis_index("seq").astype(jnp.int32).reshape(1)
    rows = query_rows.shape[1]
    sources = (
        place,
        query_rows[0],
        key_rows[0],
        value_rows[0],
        query_gain.reshape(1, -1),
        key_gain.reshape(1, -1),
        out_map.T,
        groups,
    )
    (early,) = pack(*sources, False)
    data = lax.all_to_all(early, "seq", split_axis=0, concat_axis=0, tiled=True)
    late = list(pack(*sources, True))
    late[2], late[1], data = lax.optimization_barrier((late[2], late[1], data))
    held = {0: late[0]}
    for e in (4, 5, 6, 7, 3, 2, 1):
        held[e] = lax.ppermute(late[e], "seq", [(i, i ^ e) for i in range(groups)])
    term, weights = attend_early(data.reshape(groups * rows, data.shape[2]))
    terms = attend_late(place, term, weights, [held[e] for e in range(groups)])
    terms = lax.all_to_all(terms, "seq", split_axis=0, concat_axis=0, tiled=True)
    share = jnp.where(lax.axis_index("cfg") == 0, GUIDANCE, 1.0 - GUIDANCE)
    mine = jnp.sum(terms, axis=0) * share
    both = lax.all_gather(mine, "cfg", axis=0)
    next_latents, denoised = finish(step_index, both, latents.T)
    return (next_latents.T, denoised.T)


def solution(mesh):
    placed = (
        P("cfg", ("batch", "seq"), None),
        P("cfg", ("batch", "seq"), None),
        P("cfg", ("batch", "seq"), None),
        P(),
        P(),
        P(),
        P(("batch", "seq"), None),
        P(),
    )
    return jax.shard_map(
        local,
        mesh=mesh,
        in_specs=placed,
        out_specs=(P(("batch", "seq"), None), P(("batch", "seq"), None)),
        check_vma=False,
    )
```

```python
import functools
import math

import jax
import jax.numpy as jnp
from jax import lax
from jax.experimental import pallas as pl
from jax.experimental.pallas import tpu as pltpu
from jax.sharding import PartitionSpec as P

HEADS = 32
HEAD_DIM = 128
CHANNELS = 64
STEPS = 50
GUIDANCE = 5.0
FLOW_SHIFT = 5.0
EPSILON = 1e-06
VMEM_LIMIT = 24 * 1024 * 1024
PACK_VMEM_LIMIT = 60 * 1024 * 1024
PIECES = 2


def sigma_at(progress):
    remain = 1.0 - progress / STEPS
    return FLOW_SHIFT * remain / (1.0 + (FLOW_SHIFT - 1.0) * remain)


def params(limit=VMEM_LIMIT):
    return pltpu.CompilerParams(vmem_limit_bytes=limit)


def normed(values, gain):
    values = values.astype(jnp.float32)
    mean_square = jnp.mean(values * values, axis=-1, keepdims=True)
    return (values * lax.rsqrt(mean_square + EPSILON) * gain).astype(jnp.bfloat16)


def mapped_pair(values, map_ref, first):
    columns = map_ref[:, first : first + 2 * HEAD_DIM]
    none = jnp.zeros((CHANNELS, HEAD_DIM), jnp.bfloat16)
    both = jnp.concatenate(
        [
            jnp.concatenate([columns[:, :HEAD_DIM], none], axis=1),
            jnp.concatenate([none, columns[:, HEAD_DIM:]], axis=1),
        ],
        axis=0,
    )
    return lax.dot_general(
        values, both, (((1,), (1,)), ((), ())), preferred_element_type=jnp.float32
    ).astype(jnp.bfloat16)


def pack_kernel(groups, late, cuts, place_ref, *refs):
    outs = 1 if not late else groups
    sources, gains, map_hbm = refs[:3], refs[3:5], refs[5]
    out_refs = refs[6 : 6 + outs]
    held, gain_refs, map_ref, stage, in_sems, small_sems, out_sems = refs[6 + outs :]
    rows, features = sources[0].shape
    width = features // groups
    head_part = width - HEAD_DIM
    pieces = len(cuts) - 1
    small = [
        pltpu.make_async_copy(gains[0], gain_refs.at[0], small_sems.at[0]),
        pltpu.make_async_copy(gains[1], gain_refs.at[1], small_sems.at[1]),
        pltpu.make_async_copy(map_hbm, map_ref, small_sems.at[2]),
    ]
    loads = [
        [
            pltpu.make_async_copy(
                sources[which].at[pl.ds(cuts[piece], cuts[piece + 1] - cuts[piece])],
                held.at[which, pl.ds(cuts[piece], cuts[piece + 1] - cuts[piece])],
                in_sems.at[which, piece],
            )
            for which in range(3)
        ]
        for piece in range(pieces)
    ]
    for load in loads[0] + small:
        load.start()
    for piece in loads[1:]:
        for load in piece:
            load.start()
    for load in small:
        load.wait()
    place = place_ref[0]
    stores = []
    for piece in range(pieces):
        for load in loads[piece]:
            load.wait()
        at = slice(cuts[piece], cuts[piece + 1])
        query_normed = normed(held[0, at, :], gain_refs[0])
        key_normed = normed(held[1, at, :], gain_refs[1])
        for group in range(groups):
            start = group * width
            if late:
                first, last = start + head_part, start + width
                pair = start + 2 * HEAD_DIM
            else:
                first, last = start, start + head_part
                pair = start
            size = last - first
            stage[group, at, :size] = query_normed[:, first:last]
            stage[group, at, size : 2 * size] = key_normed[:, first:last]
            stage[group, at, 2 * size :] = mapped_pair(
                held[2, at, pair : pair + 2 * HEAD_DIM], map_ref, pair
            )
        there = pl.ds(cuts[piece], cuts[piece + 1] - cuts[piece])
        if late:
            for e in range(groups):
                store = pltpu.make_async_copy(
                    stage.at[jnp.bitwise_xor(place, e), there], out_refs[e].at[there], out_sems.at[piece, e]
                )
                store.start()
                stores.append(store)
        else:
            store = pltpu.make_async_copy(
                stage.at[:, there], out_refs[0].at[:, there], out_sems.at[piece, 0]
            )
            store.start()
            stores.append(store)
    for store in stores:
        store.wait()


def pack(place, query_rows, key_rows, value_rows, query_gain, key_gain, out_map, groups, late):
    rows, features = query_rows.shape
    cuts = [rows // 16 * part // PIECES * 16 for part in range(PIECES)] + [rows]
    pieces = len(cuts) - 1
    heads = features // groups // HEAD_DIM
    packed = 2 * (1 if late else heads - 1) * HEAD_DIM + 2 * CHANNELS
    hbm = pl.BlockSpec(memory_space=pltpu.HBM)
    if late:
        out_shape = [pltpu.HBM((rows, packed), jnp.bfloat16)] * groups
    else:
        out_shape = [pltpu.HBM((groups, rows, packed), jnp.bfloat16)]
    return pl.pallas_call(
        functools.partial(pack_kernel, groups, late, cuts),
        out_shape=out_shape,
        in_specs=[pl.BlockSpec(memory_space=pltpu.SMEM)] + [hbm] * 6,
        out_specs=[hbm] * len(out_shape),
        scratch_shapes=[
            pltpu.VMEM((3, rows, features), jnp.bfloat16),
            pltpu.VMEM((2, 1, features), jnp.float32),
            pltpu.VMEM((CHANNELS, features), jnp.bfloat16),
            pltpu.VMEM((groups, rows, packed), jnp.bfloat16),
            pltpu.SemaphoreType.DMA((3, pieces)),
            pltpu.SemaphoreType.DMA((3,)),
            pltpu.SemaphoreType.DMA((pieces, groups)),
        ],
        compiler_params=params(PACK_VMEM_LIMIT),
        cost_estimate=pl.CostEstimate(flops=2**28, bytes_accessed=8 * 2**20, transcendentals=0),
        name="pack_late" if late else "pack_early",
    )(place, query_rows, key_rows, value_rows, query_gain, key_gain, out_map)


def scores_between(queries, keys):
    return lax.dot_general(
        queries, keys, (((1,), (1,)), ((), ())), preferred_element_type=jnp.float32
    )


def softmax_weights(scores):
    factor = math.log2(math.e) / math.sqrt(HEAD_DIM)
    top = jnp.max(scores, axis=-1, keepdims=True)
    weights = jnp.exp2((scores - top) * factor)
    return (weights * (1.0 / jnp.sum(weights, axis=-1, keepdims=True))).astype(jnp.bfloat16)


def left_half():
    return lax.broadcasted_iota(jnp.int32, (1, 2 * CHANNELS), 1) < CHANNELS


def early_kernel(chunk, data_ref, term_ref, weights_ref):
    heads = 3
    mapped = data_ref[:, 2 * heads * HEAD_DIM :]

    @pl.loop(0, data_ref.shape[0] // chunk)
    def _(index):
        rows = pl.ds(pl.multiple_of(index * chunk, chunk), chunk)
        terms = []
        for head in range(heads):
            lanes = slice(head * HEAD_DIM, (head + 1) * HEAD_DIM)
            keys = slice((heads + head) * HEAD_DIM, (heads + head + 1) * HEAD_DIM)
            weights = softmax_weights(scores_between(data_ref[rows, lanes], data_ref[:, keys]))
            if head < 2:
                terms.append(jnp.dot(weights, mapped, preferred_element_type=jnp.float32))
            else:
                weights_ref[rows, :] = weights
        term_ref[rows, :] = jnp.where(left_half(), terms[0], terms[1])


def late_kernel(chunk, groups, place_ref, term_ref, weights_ref, *refs):
    held_refs, out_ref, data_ref = refs[:groups], refs[groups], refs[groups + 1]
    part = held_refs[0].shape[0]
    place = place_ref[0]
    for e in range(groups):
        first = pl.multiple_of(jnp.bitwise_xor(place, e) * part, part)
        data_ref[pl.ds(first, part), :] = held_refs[e][...]
    half = part // 2
    mapped = data_ref[:, 2 * HEAD_DIM :]
    count = data_ref.shape[0] // chunk

    def scores_of(index):
        return scores_between(
            data_ref[index * chunk : (index + 1) * chunk, :HEAD_DIM], data_ref[:, HEAD_DIM : 2 * HEAD_DIM]
        )

    ahead = scores_of(0)
    for index in range(count):
        scores = ahead
        if index + 1 < count:
            ahead = scores_of(index + 1)
        rows = slice(index * chunk, (index + 1) * chunk)
        second = jnp.dot(weights_ref[rows, :], mapped, preferred_element_type=jnp.float32)
        third = jnp.dot(softmax_weights(scores), mapped, preferred_element_type=jnp.float32)
        total = term_ref[rows, :] + jnp.where(left_half(), second, third)
        total = total + pltpu.roll(total, CHANNELS, 1)
        for block in range(chunk // part):
            first = block * part
            out_ref[index * (chunk // part) + block] = jnp.where(
                left_half(), total[first : first + half], total[first + half : first + part]
            )


def attend_early(data, chunk=320):
    keys = data.shape[0]
    vmem = pl.BlockSpec(memory_space=pltpu.VMEM)
    return pl.pallas_call(
        functools.partial(early_kernel, chunk),
        out_shape=[
            jax.ShapeDtypeStruct((keys, 2 * CHANNELS), jnp.float32),
            jax.ShapeDtypeStruct((keys, keys), jnp.bfloat16),
        ],
        in_specs=[vmem],
        out_specs=[vmem, vmem],
        compiler_params=params(),
        cost_estimate=pl.CostEstimate(
            flops=8 * 10**9, bytes_accessed=2 * data.size, transcendentals=3 * keys * keys
        ),
        name="attend_early",
    )(data)


def attend_late(place, term, weights, held, chunk=320):
    groups = len(held)
    part, width = held[0].shape
    vmem = pl.BlockSpec(memory_space=pltpu.VMEM)
    return pl.pallas_call(
        functools.partial(late_kernel, chunk, groups),
        out_shape=jax.ShapeDtypeStruct((groups, part // 2, 2 * CHANNELS), jnp.float32),
        in_specs=[pl.BlockSpec(memory_space=pltpu.SMEM)] + [vmem] * (groups + 2),
        out_specs=vmem,
        scratch_shapes=[pltpu.VMEM((groups * part, width), jnp.bfloat16)],
        compiler_params=params(),
        cost_estimate=pl.CostEstimate(
            flops=3 * 10**9, bytes_accessed=2 * 10**6, transcendentals=(groups * part) ** 2
        ),
        name="attend_late",
    )(place, term, weights, *held)


def finish_kernel(index_ref, both_ref, latents_ref, next_ref, denoised_ref):
    progress = index_ref[0].astype(jnp.float32)
    sigma_now = sigma_at(progress)
    sigma_next = sigma_at(progress + 1.0)
    turned = (both_ref[0] + both_ref[1]).T
    guided = jnp.concatenate([turned[:CHANNELS], turned[CHANNELS:]], axis=1)
    latents = latents_ref[...]
    next_ref[...] = latents + (sigma_next - sigma_now) * guided
    denoised_ref[...] = latents - sigma_now * guided


def finish(step_index, both, latents):
    vmem = pl.BlockSpec(memory_space=pltpu.VMEM)
    return pl.pallas_call(
        finish_kernel,
        out_shape=[jax.ShapeDtypeStruct(latents.shape, latents.dtype)] * 2,
        in_specs=[pl.BlockSpec(memory_space=pltpu.SMEM), vmem, vmem],
        out_specs=[vmem, vmem],
        compiler_params=params(),
        cost_estimate=pl.CostEstimate(flops=2**16, bytes_accessed=2**17, transcendentals=0),
        name="finish",
    )(step_index, both, latents)


def local(query_rows, key_rows, value_rows, query_gain, key_gain, out_map, latents, step_index):
    groups = lax.axis_size("seq")
    place = lax.axis_index("seq").astype(jnp.int32).reshape(1)
    rows = query_rows.shape[1]
    sources = (
        place,
        query_rows[0],
        key_rows[0],
        value_rows[0],
        query_gain.reshape(1, -1),
        key_gain.reshape(1, -1),
        out_map.T,
        groups,
    )
    (early,) = pack(*sources, False)
    data = lax.all_to_all(early, "seq", split_axis=0, concat_axis=0, tiled=True)
    late = list(pack(*sources, True))
    late[3], late[2], data = lax.optimization_barrier((late[3], late[2], data))
    held = {0: late[0]}
    for e in (1, 4, 5, 6, 7, 2, 3):
        held[e] = lax.ppermute(late[e], "seq", [(i, i ^ e) for i in range(groups)])
    term, weights = attend_early(data.reshape(groups * rows, data.shape[2]))
    terms = attend_late(place, term, weights, [held[e] for e in range(groups)])
    terms = lax.all_to_all(terms, "seq", split_axis=0, concat_axis=0, tiled=True)
    share = jnp.where(lax.axis_index("cfg") == 0, GUIDANCE, 1.0 - GUIDANCE)
    mine = jnp.sum(terms, axis=0) * share
    both = lax.all_gather(mine, "cfg", axis=0)
    next_latents, denoised = finish(step_index, both, latents.T)
    return (next_latents.T, denoised.T)


def solution(mesh):
    placed = (
        P("cfg", ("batch", "seq"), None),
        P("cfg", ("batch", "seq"), None),
        P("cfg", ("batch", "seq"), None),
        P(),
        P(),
        P(),
        P(("batch", "seq"), None),
        P(),
    )
    return jax.shard_map(
        local,
        mesh=mesh,
        in_specs=placed,
        out_specs=(P(("batch", "seq"), None), P(("batch", "seq"), None)),
        check_vma=False,
    )
```

```python
import functools
import math

import jax
import jax.numpy as jnp
from jax import lax
from jax.experimental import pallas as pl
from jax.experimental.pallas import tpu as pltpu
from jax.sharding import PartitionSpec as P

HEADS = 32
HEAD_DIM = 128
CHANNELS = 64
STEPS = 50
GUIDANCE = 5.0
FLOW_SHIFT = 5.0
EPSILON = 1e-06
VMEM_LIMIT = 24 * 1024 * 1024
PACK_VMEM_LIMIT = 60 * 1024 * 1024
PIECES = 2


def sigma_at(progress):
    remain = 1.0 - progress / STEPS
    return FLOW_SHIFT * remain / (1.0 + (FLOW_SHIFT - 1.0) * remain)


def params(limit=VMEM_LIMIT):
    return pltpu.CompilerParams(vmem_limit_bytes=limit)


def normed(values, gain):
    values = values.astype(jnp.float32)
    mean_square = jnp.mean(values * values, axis=-1, keepdims=True)
    return (values * lax.rsqrt(mean_square + EPSILON) * gain).astype(jnp.bfloat16)


def mapped_pair(values, map_ref, first):
    columns = map_ref[:, first : first + 2 * HEAD_DIM]
    none = jnp.zeros((CHANNELS, HEAD_DIM), jnp.bfloat16)
    both = jnp.concatenate(
        [
            jnp.concatenate([columns[:, :HEAD_DIM], none], axis=1),
            jnp.concatenate([none, columns[:, HEAD_DIM:]], axis=1),
        ],
        axis=0,
    )
    return lax.dot_general(
        values, both, (((1,), (1,)), ((), ())), preferred_element_type=jnp.float32
    ).astype(jnp.bfloat16)


def pack_kernel(groups, late, cuts, place_ref, *refs):
    outs = 1 if not late else groups
    sources, gains, map_hbm = refs[:3], refs[3:5], refs[5]
    out_refs = refs[6 : 6 + outs]
    held, gain_refs, map_ref, stage, in_sems, small_sems, out_sems = refs[6 + outs :]
    rows, features = sources[0].shape
    width = features // groups
    head_part = width - HEAD_DIM
    pieces = len(cuts) - 1
    small = [
        pltpu.make_async_copy(gains[0], gain_refs.at[0], small_sems.at[0]),
        pltpu.make_async_copy(gains[1], gain_refs.at[1], small_sems.at[1]),
        pltpu.make_async_copy(map_hbm, map_ref, small_sems.at[2]),
    ]
    loads = [
        [
            pltpu.make_async_copy(
                sources[which].at[pl.ds(cuts[piece], cuts[piece + 1] - cuts[piece])],
                held.at[which, pl.ds(cuts[piece], cuts[piece + 1] - cuts[piece])],
                in_sems.at[which, piece],
            )
            for which in range(3)
        ]
        for piece in range(pieces)
    ]
    for load in loads[0] + small:
        load.start()
    for piece in loads[1:]:
        for load in piece:
            load.start()
    for load in small:
        load.wait()
    place = place_ref[0]
    stores = []
    for piece in range(pieces):
        for load in loads[piece]:
            load.wait()
        at = slice(cuts[piece], cuts[piece + 1])
        query_normed = normed(held[0, at, :], gain_refs[0])
        key_normed = normed(held[1, at, :], gain_refs[1])
        for group in range(groups):
            start = group * width
            if late:
                first, last = start + head_part, start + width
                pair = start + 2 * HEAD_DIM
            else:
                first, last = start, start + head_part
                pair = start
            size = last - first
            stage[group, at, :size] = query_normed[:, first:last]
            stage[group, at, size : 2 * size] = key_normed[:, first:last]
            stage[group, at, 2 * size :] = mapped_pair(
                held[2, at, pair : pair + 2 * HEAD_DIM], map_ref, pair
            )
        there = pl.ds(cuts[piece], cuts[piece + 1] - cuts[piece])
        if late:
            for e in range(groups):
                store = pltpu.make_async_copy(
                    stage.at[jnp.bitwise_xor(place, e), there], out_refs[e].at[there], out_sems.at[piece, e]
                )
                store.start()
                stores.append(store)
        else:
            store = pltpu.make_async_copy(
                stage.at[:, there], out_refs[0].at[:, there], out_sems.at[piece, 0]
            )
            store.start()
            stores.append(store)
    for store in stores:
        store.wait()


def pack(place, query_rows, key_rows, value_rows, query_gain, key_gain, out_map, groups, late):
    rows, features = query_rows.shape
    cuts = [rows // 16 * part // PIECES * 16 for part in range(PIECES)] + [rows]
    pieces = len(cuts) - 1
    heads = features // groups // HEAD_DIM
    packed = 2 * (1 if late else heads - 1) * HEAD_DIM + 2 * CHANNELS
    hbm = pl.BlockSpec(memory_space=pltpu.HBM)
    if late:
        out_shape = [pltpu.HBM((rows, packed), jnp.bfloat16)] * groups
    else:
        out_shape = [pltpu.HBM((groups, rows, packed), jnp.bfloat16)]
    return pl.pallas_call(
        functools.partial(pack_kernel, groups, late, cuts),
        out_shape=out_shape,
        in_specs=[pl.BlockSpec(memory_space=pltpu.SMEM)] + [hbm] * 6,
        out_specs=[hbm] * len(out_shape),
        scratch_shapes=[
            pltpu.VMEM((3, rows, features), jnp.bfloat16),
            pltpu.VMEM((2, 1, features), jnp.float32),
            pltpu.VMEM((CHANNELS, features), jnp.bfloat16),
            pltpu.VMEM((groups, rows, packed), jnp.bfloat16),
            pltpu.SemaphoreType.DMA((3, pieces)),
            pltpu.SemaphoreType.DMA((3,)),
            pltpu.SemaphoreType.DMA((pieces, groups)),
        ],
        compiler_params=params(PACK_VMEM_LIMIT),
        cost_estimate=pl.CostEstimate(flops=2**28, bytes_accessed=8 * 2**20, transcendentals=0),
        name="pack_late" if late else "pack_early",
    )(place, query_rows, key_rows, value_rows, query_gain, key_gain, out_map)


def scores_between(queries, keys):
    return lax.dot_general(
        queries, keys, (((1,), (1,)), ((), ())), preferred_element_type=jnp.float32
    )


def softmax_weights(scores):
    factor = math.log2(math.e) / math.sqrt(HEAD_DIM)
    top = jnp.max(scores, axis=-1, keepdims=True)
    weights = jnp.exp2((scores - top) * factor)
    return (weights * (1.0 / jnp.sum(weights, axis=-1, keepdims=True))).astype(jnp.bfloat16)


def left_half():
    return lax.broadcasted_iota(jnp.int32, (1, 2 * CHANNELS), 1) < CHANNELS


def early_kernel(chunk, data_ref, term_ref, weights_ref):
    heads = 3
    mapped = data_ref[:, 2 * heads * HEAD_DIM :]

    @pl.loop(0, data_ref.shape[0] // chunk)
    def _(index):
        rows = pl.ds(pl.multiple_of(index * chunk, chunk), chunk)
        terms = []
        for head in range(heads):
            lanes = slice(head * HEAD_DIM, (head + 1) * HEAD_DIM)
            keys = slice((heads + head) * HEAD_DIM, (heads + head + 1) * HEAD_DIM)
            weights = softmax_weights(scores_between(data_ref[rows, lanes], data_ref[:, keys]))
            if head < 2:
                terms.append(jnp.dot(weights, mapped, preferred_element_type=jnp.float32))
            else:
                weights_ref[rows, :] = weights
        term_ref[rows, :] = jnp.where(left_half(), terms[0], terms[1])


def late_kernel(chunk, groups, place_ref, term_ref, weights_ref, *refs):
    held_refs, out_ref, data_ref = refs[:groups], refs[groups], refs[groups + 1]
    part = held_refs[0].shape[0]
    place = place_ref[0]
    for e in range(groups):
        first = pl.multiple_of(jnp.bitwise_xor(place, e) * part, part)
        data_ref[pl.ds(first, part), :] = held_refs[e][...]
    half = part // 2
    mapped = data_ref[:, 2 * HEAD_DIM :]
    count = data_ref.shape[0] // chunk

    def scores_of(index):
        return scores_between(
            data_ref[index * chunk : (index + 1) * chunk, :HEAD_DIM], data_ref[:, HEAD_DIM : 2 * HEAD_DIM]
        )

    ahead = scores_of(0)
    for index in range(count):
        scores = ahead
        if index + 1 < count:
            ahead = scores_of(index + 1)
        rows = slice(index * chunk, (index + 1) * chunk)
        second = jnp.dot(weights_ref[rows, :], mapped, preferred_element_type=jnp.float32)
        third = jnp.dot(softmax_weights(scores), mapped, preferred_element_type=jnp.float32)
        total = term_ref[rows, :] + jnp.where(left_half(), second, third)
        total = total + pltpu.roll(total, CHANNELS, 1)
        for block in range(chunk // part):
            first = block * part
            out_ref[index * (chunk // part) + block] = jnp.where(
                left_half(), total[first : first + half], total[first + half : first + part]
            )


def attend_early(data, chunk=320):
    keys = data.shape[0]
    vmem = pl.BlockSpec(memory_space=pltpu.VMEM)
    return pl.pallas_call(
        functools.partial(early_kernel, chunk),
        out_shape=[
            jax.ShapeDtypeStruct((keys, 2 * CHANNELS), jnp.float32),
            jax.ShapeDtypeStruct((keys, keys), jnp.bfloat16),
        ],
        in_specs=[vmem],
        out_specs=[vmem, vmem],
        compiler_params=params(),
        cost_estimate=pl.CostEstimate(
            flops=8 * 10**9, bytes_accessed=2 * data.size, transcendentals=3 * keys * keys
        ),
        name="attend_early",
    )(data)


def attend_late(place, term, weights, held, chunk=320):
    groups = len(held)
    part, width = held[0].shape
    vmem = pl.BlockSpec(memory_space=pltpu.VMEM)
    return pl.pallas_call(
        functools.partial(late_kernel, chunk, groups),
        out_shape=jax.ShapeDtypeStruct((groups, part // 2, 2 * CHANNELS), jnp.float32),
        in_specs=[pl.BlockSpec(memory_space=pltpu.SMEM)] + [vmem] * (groups + 2),
        out_specs=vmem,
        scratch_shapes=[pltpu.VMEM((groups * part, width), jnp.bfloat16)],
        compiler_params=params(),
        cost_estimate=pl.CostEstimate(
            flops=3 * 10**9, bytes_accessed=2 * 10**6, transcendentals=(groups * part) ** 2
        ),
        name="attend_late",
    )(place, term, weights, *held)


def finish_kernel(index_ref, both_ref, latents_ref, next_ref, denoised_ref):
    progress = index_ref[0].astype(jnp.float32)
    sigma_now = sigma_at(progress)
    sigma_next = sigma_at(progress + 1.0)
    turned = (both_ref[0] + both_ref[1]).T
    guided = jnp.concatenate([turned[:CHANNELS], turned[CHANNELS:]], axis=1)
    latents = latents_ref[...]
    next_ref[...] = latents + (sigma_next - sigma_now) * guided
    denoised_ref[...] = latents - sigma_now * guided


def finish(step_index, both, latents):
    vmem = pl.BlockSpec(memory_space=pltpu.VMEM)
    return pl.pallas_call(
        finish_kernel,
        out_shape=[jax.ShapeDtypeStruct(latents.shape, latents.dtype)] * 2,
        in_specs=[pl.BlockSpec(memory_space=pltpu.SMEM), vmem, vmem],
        out_specs=[vmem, vmem],
        compiler_params=params(),
        cost_estimate=pl.CostEstimate(flops=2**16, bytes_accessed=2**17, transcendentals=0),
        name="finish",
    )(step_index, both, latents)


def local(query_rows, key_rows, value_rows, query_gain, key_gain, out_map, latents, step_index):
    groups = lax.axis_size("seq")
    place = lax.axis_index("seq").astype(jnp.int32).reshape(1)
    rows = query_rows.shape[1]
    sources = (
        place,
        query_rows[0],
        key_rows[0],
        value_rows[0],
        query_gain.reshape(1, -1),
        key_gain.reshape(1, -1),
        out_map.T,
        groups,
    )
    (early,) = pack(*sources, False)
    data = lax.all_to_all(early, "seq", split_axis=0, concat_axis=0, tiled=True)
    late = list(pack(*sources, True))
    term, weights = attend_early(data.reshape(groups * rows, data.shape[2]))
    late[2], late[3], term = lax.optimization_barrier((late[2], late[3], term))
    held = {0: late[0]}
    for e in (1, 4, 5, 6, 7, 2, 3):
        held[e] = lax.ppermute(late[e], "seq", [(i, i ^ e) for i in range(groups)])
    terms = attend_late(place, term, weights, [held[e] for e in range(groups)])
    terms = lax.all_to_all(terms, "seq", split_axis=0, concat_axis=0, tiled=True)
    share = jnp.where(lax.axis_index("cfg") == 0, GUIDANCE, 1.0 - GUIDANCE)
    mine = jnp.sum(terms, axis=0) * share
    both = lax.all_gather(mine, "cfg", axis=0)
    next_latents, denoised = finish(step_index, both, latents.T)
    return (next_latents.T, denoised.T)


def solution(mesh):
    placed = (
        P("cfg", ("batch", "seq"), None),
        P("cfg", ("batch", "seq"), None),
        P("cfg", ("batch", "seq"), None),
        P(),
        P(),
        P(),
        P(("batch", "seq"), None),
        P(),
    )
    return jax.shard_map(
        local,
        mesh=mesh,
        in_specs=placed,
        out_specs=(P(("batch", "seq"), None), P(("batch", "seq"), None)),
        check_vma=False,
    )
```

```python
import functools
import math

import jax
import jax.numpy as jnp
from jax import lax
from jax.experimental import pallas as pl
from jax.experimental.pallas import tpu as pltpu
from jax.sharding import PartitionSpec as P

HEADS = 32
HEAD_DIM = 128
CHANNELS = 64
STEPS = 50
GUIDANCE = 5.0
FLOW_SHIFT = 5.0
EPSILON = 1e-06
VMEM_LIMIT = 24 * 1024 * 1024
PACK_VMEM_LIMIT = 60 * 1024 * 1024
PIECES = 2


def sigma_at(progress):
    remain = 1.0 - progress / STEPS
    return FLOW_SHIFT * remain / (1.0 + (FLOW_SHIFT - 1.0) * remain)


def params(limit=VMEM_LIMIT):
    return pltpu.CompilerParams(vmem_limit_bytes=limit)


def normed(values, gain):
    values = values.astype(jnp.float32)
    mean_square = jnp.mean(values * values, axis=-1, keepdims=True)
    return (values * lax.rsqrt(mean_square + EPSILON) * gain).astype(jnp.bfloat16)


def mapped_pair(values, map_ref, first):
    columns = map_ref[:, first : first + 2 * HEAD_DIM]
    none = jnp.zeros((CHANNELS, HEAD_DIM), jnp.bfloat16)
    both = jnp.concatenate(
        [
            jnp.concatenate([columns[:, :HEAD_DIM], none], axis=1),
            jnp.concatenate([none, columns[:, HEAD_DIM:]], axis=1),
        ],
        axis=0,
    )
    return lax.dot_general(
        values, both, (((1,), (1,)), ((), ())), preferred_element_type=jnp.float32
    ).astype(jnp.bfloat16)


def pack_kernel(groups, late, cuts, place_ref, *refs):
    outs = 1 if not late else groups
    sources, gains, map_hbm = refs[:3], refs[3:5], refs[5]
    out_refs = refs[6 : 6 + outs]
    held, gain_refs, map_ref, stage, in_sems, small_sems, out_sems = refs[6 + outs :]
    rows, features = sources[0].shape
    width = features // groups
    head_part = width - HEAD_DIM
    pieces = len(cuts) - 1
    small = [
        pltpu.make_async_copy(gains[0], gain_refs.at[0], small_sems.at[0]),
        pltpu.make_async_copy(gains[1], gain_refs.at[1], small_sems.at[1]),
        pltpu.make_async_copy(map_hbm, map_ref, small_sems.at[2]),
    ]
    loads = [
        [
            pltpu.make_async_copy(
                sources[which].at[pl.ds(cuts[piece], cuts[piece + 1] - cuts[piece])],
                held.at[which, pl.ds(cuts[piece], cuts[piece + 1] - cuts[piece])],
                in_sems.at[which, piece],
            )
            for which in range(3)
        ]
        for piece in range(pieces)
    ]
    for load in loads[0] + small:
        load.start()
    for piece in loads[1:]:
        for load in piece:
            load.start()
    for load in small:
        load.wait()
    place = place_ref[0]
    stores = []
    for piece in range(pieces):
        for load in loads[piece]:
            load.wait()
        at = slice(cuts[piece], cuts[piece + 1])
        query_normed = normed(held[0, at, :], gain_refs[0])
        key_normed = normed(held[1, at, :], gain_refs[1])
        for group in range(groups):
            start = group * width
            if late:
                first, last = start + head_part, start + width
                pair = start + 2 * HEAD_DIM
            else:
                first, last = start, start + head_part
                pair = start
            size = last - first
            stage[group, at, :size] = query_normed[:, first:last]
            stage[group, at, size : 2 * size] = key_normed[:, first:last]
            stage[group, at, 2 * size :] = mapped_pair(
                held[2, at, pair : pair + 2 * HEAD_DIM], map_ref, pair
            )
        there = pl.ds(cuts[piece], cuts[piece + 1] - cuts[piece])
        if late:
            for e in range(groups):
                store = pltpu.make_async_copy(
                    stage.at[jnp.bitwise_xor(place, e), there], out_refs[e].at[there], out_sems.at[piece, e]
                )
                store.start()
                stores.append(store)
        else:
            store = pltpu.make_async_copy(
                stage.at[:, there], out_refs[0].at[:, there], out_sems.at[piece, 0]
            )
            store.start()
            stores.append(store)
    for store in stores:
        store.wait()


def pack(place, query_rows, key_rows, value_rows, query_gain, key_gain, out_map, groups, late):
    rows, features = query_rows.shape
    cuts = [rows // 16 * part // PIECES * 16 for part in range(PIECES)] + [rows]
    pieces = len(cuts) - 1
    heads = features // groups // HEAD_DIM
    packed = 2 * (1 if late else heads - 1) * HEAD_DIM + 2 * CHANNELS
    hbm = pl.BlockSpec(memory_space=pltpu.HBM)
    if late:
        out_shape = [pltpu.HBM((rows, packed), jnp.bfloat16)] * groups
    else:
        out_shape = [pltpu.HBM((groups, rows, packed), jnp.bfloat16)]
    return pl.pallas_call(
        functools.partial(pack_kernel, groups, late, cuts),
        out_shape=out_shape,
        in_specs=[pl.BlockSpec(memory_space=pltpu.SMEM)] + [hbm] * 6,
        out_specs=[hbm] * len(out_shape),
        scratch_shapes=[
            pltpu.VMEM((3, rows, features), jnp.bfloat16),
            pltpu.VMEM((2, 1, features), jnp.float32),
            pltpu.VMEM((CHANNELS, features), jnp.bfloat16),
            pltpu.VMEM((groups, rows, packed), jnp.bfloat16),
            pltpu.SemaphoreType.DMA((3, pieces)),
            pltpu.SemaphoreType.DMA((3,)),
            pltpu.SemaphoreType.DMA((pieces, groups)),
        ],
        compiler_params=params(PACK_VMEM_LIMIT),
        cost_estimate=pl.CostEstimate(flops=2**28, bytes_accessed=8 * 2**20, transcendentals=0),
        name="pack_late" if late else "pack_early",
    )(place, query_rows, key_rows, value_rows, query_gain, key_gain, out_map)


def scores_between(queries, keys):
    return lax.dot_general(
        queries, keys, (((1,), (1,)), ((), ())), preferred_element_type=jnp.float32
    )


def softmax_weights(scores):
    factor = math.log2(math.e) / math.sqrt(HEAD_DIM)
    top = jnp.max(scores, axis=-1, keepdims=True)
    weights = jnp.exp2((scores - top) * factor)
    return (weights * (1.0 / jnp.sum(weights, axis=-1, keepdims=True))).astype(jnp.bfloat16)


def left_half():
    return lax.broadcasted_iota(jnp.int32, (1, 2 * CHANNELS), 1) < CHANNELS


def early_kernel(chunk, whole, data_ref, out_ref):
    heads = 3
    mapped = data_ref[:, 2 * heads * HEAD_DIM :]
    steps = [
        (slice(first, first + chunk), head)
        for first in range(0, data_ref.shape[0], chunk)
        for head in ((0, 1) if whole else (2,))
    ]

    def scores_of(rows, head):
        lanes = slice(head * HEAD_DIM, (head + 1) * HEAD_DIM)
        keys = slice((heads + head) * HEAD_DIM, (heads + head + 1) * HEAD_DIM)
        return scores_between(data_ref[rows, lanes], data_ref[:, keys])

    ahead = scores_of(*steps[0])
    kept = None
    for index, (rows, head) in enumerate(steps):
        scores = ahead
        if index + 1 < len(steps):
            ahead = scores_of(*steps[index + 1])
        weights = softmax_weights(scores)
        if not whole:
            out_ref[rows, :] = weights
            continue
        term = jnp.dot(weights, mapped, preferred_element_type=jnp.float32)
        if head == 0:
            kept = term
        else:
            out_ref[rows, :] = jnp.where(left_half(), kept, term)


def late_kernel(chunk, groups, place_ref, term_ref, weights_ref, *refs):
    held_refs, out_ref, data_ref = refs[:groups], refs[groups], refs[groups + 1]
    part = held_refs[0].shape[0]
    place = place_ref[0]
    for e in range(groups):
        first = pl.multiple_of(jnp.bitwise_xor(place, e) * part, part)
        data_ref[pl.ds(first, part), :] = held_refs[e][...]
    half = part // 2
    mapped = data_ref[:, 2 * HEAD_DIM :]
    count = data_ref.shape[0] // chunk

    def scores_of(index):
        return scores_between(
            data_ref[index * chunk : (index + 1) * chunk, :HEAD_DIM], data_ref[:, HEAD_DIM : 2 * HEAD_DIM]
        )

    ahead = scores_of(0)
    for index in range(count):
        scores = ahead
        if index + 1 < count:
            ahead = scores_of(index + 1)
        rows = slice(index * chunk, (index + 1) * chunk)
        second = jnp.dot(weights_ref[rows, :], mapped, preferred_element_type=jnp.float32)
        third = jnp.dot(softmax_weights(scores), mapped, preferred_element_type=jnp.float32)
        total = term_ref[rows, :] + jnp.where(left_half(), second, third)
        total = total + pltpu.roll(total, CHANNELS, 1)
        for block in range(chunk // part):
            first = block * part
            out_ref[index * (chunk // part) + block] = jnp.where(
                left_half(), total[first : first + half], total[first + half : first + part]
            )


def attend_early(data, whole, chunk=320):
    keys = data.shape[0]
    vmem = pl.BlockSpec(memory_space=pltpu.VMEM)
    if whole:
        out_shape = jax.ShapeDtypeStruct((keys, 2 * CHANNELS), jnp.float32)
    else:
        out_shape = jax.ShapeDtypeStruct((keys, keys), jnp.bfloat16)
    return pl.pallas_call(
        functools.partial(early_kernel, chunk, whole),
        out_shape=out_shape,
        in_specs=[vmem],
        out_specs=vmem,
        compiler_params=params(),
        cost_estimate=pl.CostEstimate(
            flops=4 * 10**9, bytes_accessed=2 * data.size, transcendentals=keys * keys
        ),
        name="attend_early",
    )(data)


def attend_late(place, term, weights, held, chunk=320):
    groups = len(held)
    part, width = held[0].shape
    vmem = pl.BlockSpec(memory_space=pltpu.VMEM)
    return pl.pallas_call(
        functools.partial(late_kernel, chunk, groups),
        out_shape=jax.ShapeDtypeStruct((groups, part // 2, 2 * CHANNELS), jnp.float32),
        in_specs=[pl.BlockSpec(memory_space=pltpu.SMEM)] + [vmem] * (groups + 2),
        out_specs=vmem,
        scratch_shapes=[pltpu.VMEM((groups * part, width), jnp.bfloat16)],
        compiler_params=params(),
        cost_estimate=pl.CostEstimate(
            flops=3 * 10**9, bytes_accessed=2 * 10**6, transcendentals=(groups * part) ** 2
        ),
        name="attend_late",
    )(place, term, weights, *held)


def finish_kernel(index_ref, both_ref, latents_ref, next_ref, denoised_ref):
    progress = index_ref[0].astype(jnp.float32)
    sigma_now = sigma_at(progress)
    sigma_next = sigma_at(progress + 1.0)
    turned = (both_ref[0] + both_ref[1]).T
    guided = jnp.concatenate([turned[:CHANNELS], turned[CHANNELS:]], axis=1)
    latents = latents_ref[...]
    next_ref[...] = latents + (sigma_next - sigma_now) * guided
    denoised_ref[...] = latents - sigma_now * guided


def finish(step_index, both, latents):
    vmem = pl.BlockSpec(memory_space=pltpu.VMEM)
    return pl.pallas_call(
        finish_kernel,
        out_shape=[jax.ShapeDtypeStruct(latents.shape, latents.dtype)] * 2,
        in_specs=[pl.BlockSpec(memory_space=pltpu.SMEM), vmem, vmem],
        out_specs=[vmem, vmem],
        compiler_params=params(),
        cost_estimate=pl.CostEstimate(flops=2**16, bytes_accessed=2**17, transcendentals=0),
        name="finish",
    )(step_index, both, latents)


def local(query_rows, key_rows, value_rows, query_gain, key_gain, out_map, latents, step_index):
    groups = lax.axis_size("seq")
    place = lax.axis_index("seq").astype(jnp.int32).reshape(1)
    rows = query_rows.shape[1]
    sources = (
        place,
        query_rows[0],
        key_rows[0],
        value_rows[0],
        query_gain.reshape(1, -1),
        key_gain.reshape(1, -1),
        out_map.T,
        groups,
    )
    (early,) = pack(*sources, False)
    data = lax.all_to_all(early, "seq", split_axis=0, concat_axis=0, tiled=True)
    late = list(pack(*sources, True))
    late[2], data = lax.optimization_barrier((late[2], data))
    flat = data.reshape(groups * rows, data.shape[2])
    weights = attend_early(flat, False)
    late[3], weights, flat = lax.optimization_barrier((late[3], weights, flat))
    held = {0: late[0]}
    for e in (1, 4, 5, 6, 7, 2, 3):
        held[e] = lax.ppermute(late[e], "seq", [(i, i ^ e) for i in range(groups)])
    term = attend_early(flat, True)
    terms = attend_late(place, term, weights, [held[e] for e in range(groups)])
    terms = lax.all_to_all(terms, "seq", split_axis=0, concat_axis=0, tiled=True)
    share = jnp.where(lax.axis_index("cfg") == 0, GUIDANCE, 1.0 - GUIDANCE)
    mine = jnp.sum(terms, axis=0) * share
    both = lax.all_gather(mine, "cfg", axis=0)
    next_latents, denoised = finish(step_index, both, latents.T)
    return (next_latents.T, denoised.T)


def solution(mesh):
    placed = (
        P("cfg", ("batch", "seq"), None),
        P("cfg", ("batch", "seq"), None),
        P("cfg", ("batch", "seq"), None),
        P(),
        P(),
        P(),
        P(("batch", "seq"), None),
        P(),
    )
    return jax.shard_map(
        local,
        mesh=mesh,
        in_specs=placed,
        out_specs=(P(("batch", "seq"), None), P(("batch", "seq"), None)),
        check_vma=False,
    )
```
